32 devices in a mesh: sec: 8 (over y, x, core), tile: 4 (over z).
Axes of the slice: x: 2, y: 2, z: 4, core: 2. Of those that a mesh axis runs over, the one named last changes fastest.
Arguments:
- displacement: float32 [2, 16, 32, 2048], P(None, 'sec', 'tile'), may hold values from -6 to 6
- velocity: float32 [2, 16, 32, 2048], P(None, 'sec', 'tile'), may hold values from -10 to 10
- frac: bfloat16 [2, 4, 16, 32, 2048], P(None, None, 'sec', 'tile'), may hold values from 0 to 1
- offsets: int32 [4, 16, 4, 2], P(None, 'sec', 'tile'), may hold values from -2 to 2
- fixed: int32 [16, 32, 2048], P('sec', 'tile'), may hold values 0 or 1
- trans: float32 [16, 2], P('sec'), may hold values from -0.3 to 0.3
Outputs:
- new_displacement: float32 [2, 16, 32, 2048], P(None, 'sec', 'tile')
- new_velocity: float32 [2, 16, 32, 2048], P(None, 'sec', 'tile')
The draws below stay inside these ranges and needn't reach their ends.
All inputs are finite; a program needn't handle non-finite values. No bound on the sum of `fixed` on one device may be relied on, other than what follows from the above.
Results may differ from the reference program's by a relative error of at most 0.0003.
Values sent between devices are 32-bit elements; how exact they have to be, the bound alone decides.
A program may use at most 64 MiB of HBM per device.

```python
import jax
import jax.numpy as jnp
from jax import lax

TR = 8
COLS = 2048
ITERS = 3
SECTIONS = 16
TILES = 4
ROWS = 32


def draw_velocity(key, part):
    sec_scale = 0.4 + 1.2 * jnp.arange(SECTIONS, dtype=jnp.float32) / SECTIONS
    row_scale = 0.5 + jnp.arange(ROWS, dtype=jnp.float32) / ROWS
    scale = sec_scale[:, None, None] * row_scale[None, :, None]
    base = jnp.clip(jax.random.normal(key, (2, SECTIONS, ROWS, COLS), jnp.float32), -4.0, 4.0)
    return base * scale[None]


def place_ends(entries, rng, least, top_value):
    spot = [jax.random.randint(jax.random.fold_in(rng, axis), (), 0, length) for axis, length in enumerate(entries.shape)]
    longest = entries.shape.index(max(entries.shape))
    beside = spot[:longest] + [(spot[longest] + 1) % entries.shape[longest]] + spot[longest + 1:]
    return entries.at[tuple(spot)].set(least).at[tuple(beside)].set(top_value)


def levels(rng, shape, pieces, low, high):
    def one(position, shards_of):
        heights = jax.random.uniform(jax.random.fold_in(jax.random.fold_in(rng, 6), position), (shards_of,), jnp.float32, low / len(pieces), high / len(pieces))
        return jnp.repeat(jnp.exp(heights), shape[position] // shards_of).reshape((-1,) + (1,) * (len(shape) - position - 1))

    factor_of = one(*pieces[0])
    for cut in pieces[1:]:
        factor_of = factor_of * one(*cut)
    return factor_of


def bell_draw(own_key, extent, scale, limit, split=(), kind=jnp.bfloat16):
    result = jax.random.normal(own_key, extent, jnp.float32) * scale
    if len(split) > 0:
        result = levels(own_key, extent, split, -0.22, 0.18) * result
    return jnp.clip(result, min=-limit, max=limit).astype(kind)


def setup_inputs(seed: int = 0) -> dict:
    streams_of = jax.random.split(jax.random.key(seed), 7)
    return {
        "displacement": bell_draw(streams_of[0], (2, SECTIONS, ROWS, COLS), 1.0, 6.0, ((1, 8), (2, 4)), jnp.float32),
        "velocity": draw_velocity(jax.random.fold_in(streams_of[6], 71), 0),
        "frac": jnp.clip(1.0 * jax.random.uniform(streams_of[2], (2, 4, SECTIONS, ROWS, COLS), jnp.float32) ** levels(streams_of[2], (2, 4, SECTIONS, ROWS, COLS), ((2, 8), (3, 4)), -0.2, 0.2), 0.0, 1.0).astype(jnp.bfloat16),
        "offsets": place_ends(jax.random.randint(streams_of[3], (4, SECTIONS, TILES, 2), -2, 3), jax.random.fold_in(streams_of[3], 1), -2, 2).astype(jnp.int32),
        "fixed": place_ends((jax.random.randint(streams_of[4], (SECTIONS, ROWS, COLS), 0, 16) < 1).astype(jnp.int32), jax.random.fold_in(streams_of[4], 1), 0, 1),
        "trans": jnp.clip(jax.random.uniform(streams_of[5], (SECTIONS, 2), jnp.float32, -0.3, 0.3) * levels(streams_of[5], (SECTIONS, 2), ((0, 8),), -0.4, 0.0), -0.3, 0.3),
    }


in_stiff = 1.0
anchor_stiff = 0.25
cross_stiff = (0.25, 0.5, 0.5, 0.25)
reaches = (-2, -1, 1, 2)

def spring_force(ext, frac, offsets, fixed, anchor, sec_first, row_first, sections, rows):
    count = fixed.shape[0]
    height = fixed.shape[1]
    width = fixed.shape[2]
    centre = ext[:, 2:count + 2, 3:height + 3, :]
    grow = row_first + jnp.arange(height, dtype=jnp.int32)
    gcol = jnp.arange(width, dtype=jnp.int32)
    gsec = sec_first + jnp.arange(count, dtype=jnp.int32)
    above = ext[:, 2:count + 2, 2:height + 2, :]
    below = ext[:, 2:count + 2, 4:height + 4, :]
    left = jnp.roll(centre, 1, axis=3)
    right = jnp.roll(centre, -1, axis=3)
    force = jnp.where((grow > 0)[:, None], above - centre, 0.0)
    force = force + jnp.where((grow < rows - 1)[:, None], below - centre, 0.0)
    force = force + jnp.where((gcol > 0)[None, :], left - centre, 0.0)
    force = force + jnp.where((gcol < width - 1)[None, :], right - centre, 0.0)
    force = in_stiff * force + anchor_stiff * (jnp.transpose(anchor)[:, :, None, None] - centre)
    for index in range(4):
        reach = reaches[index]
        stiff = cross_stiff[index]
        source = ext[:, 2 + reach:2 + reach + count]

        def pull(block, frow, fcol, shift, own, section):
            frow = frow.astype(jnp.float32)
            fcol = fcol.astype(jnp.float32)
            part_rows = lax.dynamic_slice_in_dim(block, 3 + shift[0], height + 1, 1)
            first = jnp.roll(part_rows, -shift[1], axis=2)
            second = jnp.roll(part_rows, -shift[1] - 1, axis=2)
            match = (1.0 - frow) * ((1.0 - fcol) * first[:, :height] + fcol * second[:, :height])
            match = match + frow * ((1.0 - fcol) * first[:, 1:] + fcol * second[:, 1:])
            flow = jnp.stack([shift[0].astype(jnp.float32) + frow, shift[1].astype(jnp.float32) + fcol])
            gap = match + flow - own
            row_ok = (grow + shift[0] >= 0) & (grow + shift[0] + 1 <= rows - 1)
            col_ok = (gcol + shift[1] >= 0) & (gcol + shift[1] + 1 <= width - 1)
            sec_ok = (section + reach >= 0) & (section + reach < sections)
            valid = row_ok[:, None] & col_ok[None, :] & sec_ok
            return jnp.where(valid, stiff * gap, 0.0)
        force = force + jax.vmap(pull, in_axes=(1, 0, 0, 0, 1, 0), out_axes=1)(source, frac[0, index], frac[1, index], offsets[index], centre, gsec)
    return force * (1 - fixed).astype(jnp.float32)[None]

def reference(displacement, velocity, frac, offsets, fixed, trans):
    anchor = jnp.cumsum(trans, 0)
    keep = (1 - fixed).astype(jnp.float32)
    moving = velocity * keep[None]
    shifted = displacement
    for step in range(ITERS):
        alpha = 0.1 * 0.99 ** step
        delta = 0.25 * 1.1 ** step
        padded = jnp.pad(shifted, ((0, 0), (2, 2), (3, 3), (0, 0)))

        def tile_force(tile_index):
            start = (tile_index * TR).astype(jnp.int32)
            ext = lax.dynamic_slice_in_dim(padded, start, TR + 6, 2)
            piece = lax.dynamic_slice_in_dim(frac, start, TR, 3)
            held = lax.dynamic_slice_in_dim(fixed, start, TR, 1)
            shift = lax.dynamic_index_in_dim(offsets, tile_index, 2, keepdims=False)
            return spring_force(ext, piece, shift, held, anchor, 0, start, SECTIONS, ROWS)
        forces = lax.map(tile_force, jnp.arange(TILES, dtype=jnp.int32))
        force = jnp.moveaxis(forces, 0, 2).reshape(2, SECTIONS, ROWS, COLS)
        ff = jnp.sum(force * force)
        vv = jnp.sum(moving * moving)
        ratio = jnp.sqrt(vv / (ff + 1e-06))
        moving = (1.0 - alpha) * moving + alpha * ratio * force
        moving = moving + delta * force
        shifted = shifted + delta * moving
    return (shifted, moving)
```

```python
import functools

import jax
import jax.numpy as jnp
from jax import lax
from jax.experimental import pallas as pl
from jax.experimental.pallas import tpu as pltpu
from jax.sharding import PartitionSpec as P

ITERS = 3
LANES = 128
UP = 2
DOWN = 3
REACH = 2

in_stiff = 1.0
anchor_stiff = 0.25
cross_stiff = (0.25, 0.5, 0.5, 0.25)
reaches = (-2, -1, 1, 2)
MESH = pl.DeviceIdType.MESH


def pick(step, values):
    chosen = jnp.float32(values[-1])
    for index in range(len(values) - 1):
        chosen = jnp.where(step == index, jnp.float32(values[index]), chosen)
    return chosen


def kernel(
    n_sec, n_tile, off_ref, u_ref, v_in, frac_ref, fixed_ref, trans_ref, u_out, v_out,
    ext, force, keep, trans_all, anchor, part, part_tile, norms_sec, norms_tile,
    halo_send, halo_recv, tr_send, tr_recv, sec_send, sec_recv, tile_send, tile_recv,
):
    _, count, height, subs, lanes = u_ref.shape
    width = subs * lanes
    sections = count * n_sec
    rows = height * n_tile
    my_sec = lax.axis_index("sec")
    my_tile = lax.axis_index("tile")
    sec_first = my_sec * count
    row_first = my_tile * height
    shape = (height, subs, lanes)
    grow = row_first + lax.broadcasted_iota(jnp.int32, shape, 0)
    lane = lax.broadcasted_iota(jnp.int32, shape, 2)
    gcol = lax.broadcasted_iota(jnp.int32, shape, 1) * lanes + lane
    lane_of = lax.broadcasted_iota(jnp.int32, (1, 1, lanes), 2)

    ways = [(a, b) for a in (-1, 0, 1) for b in (-1, 0, 1) if (a, b) != (0, 0)]
    sec_at = {-1: pl.ds(REACH + count, REACH), 0: pl.ds(REACH, count), 1: pl.ds(0, REACH)}
    sec_from = {-1: pl.ds(REACH, REACH), 0: pl.ds(REACH, count), 1: pl.ds(count, REACH)}
    row_at = {-1: pl.ds(UP + height, DOWN), 0: pl.ds(UP, height), 1: pl.ds(0, UP)}
    row_from = {-1: pl.ds(UP, DOWN), 0: pl.ds(UP, height), 1: pl.ds(height, UP)}

    def halo(way):
        a, b = ways[way]
        return pltpu.make_async_remote_copy(
            src_ref=ext.at[:, sec_from[a], row_from[b]],
            dst_ref=ext.at[:, sec_at[a], row_at[b]],
            send_sem=halo_send.at[way],
            recv_sem=halo_recv.at[way],
            device_id=(lax.rem(my_sec + a + n_sec, n_sec), lax.rem(my_tile + b + n_tile, n_tile)),
            device_id_type=MESH,
        )

    def there(a, b):
        sec_ok = (my_sec + a >= 0) & (my_sec + a < n_sec)
        return sec_ok & (my_tile + b >= 0) & (my_tile + b < n_tile)

    def send_halo():
        for way, (a, b) in enumerate(ways):
            pl.when(there(a, b))(lambda way=way: halo(way).start())

    def halo_sent():
        for way, (a, b) in enumerate(ways):
            pl.when(there(a, b))(lambda way=way: halo(way).wait_send())

    def halo_here():
        for way, (a, b) in enumerate(ways):
            pl.when(there(-a, -b))(lambda way=way: halo(way).wait_recv())

    def spread(src, slots, send, recv, n, me, peer):
        def copy(turn, place):
            return pltpu.make_async_remote_copy(
                src_ref=src,
                dst_ref=slots.at[place],
                send_sem=send.at[turn],
                recv_sem=recv.at[place],
                device_id=peer(lax.rem(me + turn, n)),
                device_id_type=MESH,
            )

        for turn in range(1, n):
            copy(turn, me).start()
        return copy

    def gathered(copy, n, me):
        for turn in range(1, n):
            copy(turn, lax.rem(me + turn, n)).wait_recv()
        for turn in range(1, n):
            copy(turn, me).wait_send()

    def along_sec(to):
        return (to, my_tile)

    def along_tile(to):
        return (my_sec, to)

    def shifted(cells, by):
        turned = pltpu.roll(cells, lax.rem(lanes - by, lanes), 2)
        after = pltpu.roll(turned, subs - 1, 1)
        before = pltpu.roll(turned, 1, 1)
        place = lane_of + by
        return jnp.where(place > lanes - 1, after, jnp.where(place < 0, before, turned))

    ext[:, REACH : REACH + count, UP : UP + height] = u_ref[...]
    send_halo()
    trans_copy = spread(trans_ref, trans_all, tr_send, tr_recv, n_sec, my_sec, along_sec)
    keep[...] = (1 - fixed_ref[...]).astype(jnp.float32)
    for c in range(2):
        v_out[c] = v_in[c] * keep[...]
    trans_all[my_sec] = trans_ref[...]
    gathered(trans_copy, n_sec, my_sec)
    before = jnp.zeros(trans_ref.shape, jnp.float32)
    for turn in range(n_sec):
        before = before + jnp.where(turn < my_sec, trans_all[turn], 0.0)
    for c in range(2):
        run = jnp.zeros((1, lanes), jnp.float32)
        for s in range(count):
            run = run + before[2 * s + c : 2 * s + c + 1]
        for s in range(count):
            run = run + trans_ref[2 * s + c : 2 * s + c + 1, :]
            anchor[2 * s + c : 2 * s + c + 1, :] = run

    def iteration(step, _):
        halo_here()
        ff = jnp.zeros((subs, lanes), jnp.float32)
        vv = jnp.zeros((subs, lanes), jnp.float32)
        for s in range(count):
            own = [ext[c, REACH + s, UP : UP + height] for c in range(2)]
            total = []
            for c in range(2):
                mid = own[c]
                above = ext[c, REACH + s, UP - 1 : UP - 1 + height]
                below = ext[c, REACH + s, UP + 1 : UP + 1 + height]
                f = jnp.where(grow > 0, above - mid, 0.0)
                f = f + jnp.where(grow < rows - 1, below - mid, 0.0)
                f = f + jnp.where(gcol > 0, shifted(mid, -1) - mid, 0.0)
                f = f + jnp.where(gcol < width - 1, shifted(mid, 1) - mid, 0.0)
                hold = anchor[2 * s + c : 2 * s + c + 1, :][None]
                total.append(in_stiff * f + anchor_stiff * (hold - mid))
            for j in range(4):
                reach = reaches[j]
                dr = off_ref[(j * count + s) * 2]
                dc = off_ref[(j * count + s) * 2 + 1]
                fr = frac_ref[0, j, s].astype(jnp.float32)
                fc = frac_ref[1, j, s].astype(jnp.float32)
                other = sec_first + s + reach
                least = jnp.where((other >= 0) & (other < sections), 0, rows + height)
                valid = (grow + dr >= least) & (grow + dr + 1 <= rows - 1)
                valid = valid & (gcol + dc >= 0) & (gcol + dc + 1 <= width - 1)
                flow = (dr.astype(jnp.float32) + fr, dc.astype(jnp.float32) + fc)
                for c in range(2):
                    near = ext[c, REACH + s + reach, pl.ds(UP + dr, height + 1)]
                    first = shifted(near, dc)
                    second = shifted(near, dc + 1)
                    top = first[:height] + fc * (second[:height] - first[:height])
                    low = first[1:] + fc * (second[1:] - first[1:])
                    match = top + fr * (low - top)
                    gap = match + flow[c] - own[c]
                    total[c] = total[c] + jnp.where(valid, cross_stiff[j] * gap, 0.0)
            for c in range(2):
                f = total[c] * keep[s]
                force[c, s] = f
                v = v_out[c, s]
                ff = ff + jnp.sum(f * f, 0)
                vv = vv + jnp.sum(v * v, 0)
        part[step, 0] = ff
        part[step, 1] = vv
        norms_sec[step, my_sec] = part[step]
        copy = spread(
            part.at[step], norms_sec.at[step], sec_send.at[step], sec_recv.at[step], n_sec, my_sec, along_sec
        )
        halo_sent()
        gathered(copy, n_sec, my_sec)
        summed = norms_sec[step, 0]
        for turn in range(1, n_sec):
            summed = summed + norms_sec[step, turn]
        part_tile[step] = summed
        norms_tile[step, my_tile] = summed
        copy = spread(
            part_tile.at[step], norms_tile.at[step], tile_send.at[step], tile_recv.at[step], n_tile, my_tile, along_tile
        )
        gathered(copy, n_tile, my_tile)
        summed = norms_tile[step, 0]
        for turn in range(1, n_tile):
            summed = summed + norms_tile[step, turn]
        all_ff = jnp.sum(summed[0], axis=(0, 1), keepdims=True)
        all_vv = jnp.sum(summed[1], axis=(0, 1), keepdims=True)
        ratio = jnp.sqrt(all_vv / (all_ff + 1e-06))
        alpha = pick(step, [0.1 * 0.99**k for k in range(ITERS)])
        delta = pick(step, [0.25 * 1.1**k for k in range(ITERS)])
        gain = jnp.broadcast_to(alpha * ratio + delta, (subs, lanes))[None]
        for c in range(2):
            for s in range(count):
                v = (1.0 - alpha) * v_out[c, s] + gain * force[c, s]
                v_out[c, s] = v
                u = ext[c, REACH + s, UP : UP + height] + delta * v
                ext[c, REACH + s, UP : UP + height] = u
        pl.when(step < ITERS - 1)(send_halo)
        return 0

    lax.fori_loop(0, ITERS, iteration, 0)
    u_out[...] = ext[:, REACH : REACH + count, UP : UP + height]


def shards(displacement, velocity, frac, offsets, fixed, trans):
    n_sec, n_tile = lax.axis_size("sec"), lax.axis_size("tile")
    _, count, height, width = displacement.shape
    subs = width // LANES
    cells = (2, count, height, subs, LANES)
    lines = -(-2 * count // 8) * 8
    shift = offsets[:, :, 0, :].reshape(-1)
    spread = jnp.broadcast_to(trans.reshape(-1, 1), (2 * count, LANES))
    spread = jnp.pad(spread, ((0, lines - 2 * count), (0, 0)))
    vmem = pl.BlockSpec(memory_space=pltpu.VMEM)
    dma = pltpu.SemaphoreType.DMA
    f32 = jnp.float32
    u, v = pl.pallas_call(
        functools.partial(kernel, n_sec, n_tile),
        out_shape=(jax.ShapeDtypeStruct(cells, f32), jax.ShapeDtypeStruct(cells, f32)),
        in_specs=[pl.BlockSpec(memory_space=pltpu.SMEM)] + [vmem] * 5,
        out_specs=(vmem, vmem),
        scratch_shapes=[
            pltpu.VMEM((2, count + 2 * REACH, height + UP + DOWN, subs, LANES), f32),
            pltpu.VMEM(cells, f32),
            pltpu.VMEM(cells[1:], f32),
            pltpu.VMEM((n_sec, lines, LANES), f32),
            pltpu.VMEM((lines, LANES), f32),
            pltpu.VMEM((ITERS, 2, subs, LANES), f32),
            pltpu.VMEM((ITERS, 2, subs, LANES), f32),
            pltpu.VMEM((ITERS, n_sec, 2, subs, LANES), f32),
            pltpu.VMEM((ITERS, n_tile, 2, subs, LANES), f32),
            dma((8,)),
            dma((8,)),
            dma((n_sec,)),
            dma((n_sec,)),
            dma((ITERS, n_sec)),
            dma((ITERS, n_sec)),
            dma((ITERS, n_tile)),
            dma((ITERS, n_tile)),
        ],
        compiler_params=pltpu.CompilerParams(has_side_effects=True, vmem_limit_bytes=40 * 2**20),
    )(
        shift,
        displacement.reshape(cells),
        velocity.reshape(cells),
        frac.reshape((2, 4) + cells[1:]),
        fixed.reshape(cells[1:]),
        spread,
    )
    return u.reshape(displacement.shape), v.reshape(displacement.shape)


def solution(mesh):
    placed = (
        P(None, "sec", "tile", None),
        P(None, "sec", "tile", None),
        P(None, None, "sec", "tile", None),
        P(None, "sec", "tile", None),
        P("sec", "tile", None),
        P("sec", None),
    )
    return jax.shard_map(
        shards,
        mesh=mesh,
        in_specs=placed,
        out_specs=(P(None, "sec", "tile", None), P(None, "sec", "tile", None)),
        check_vma=False,
    )
```

```python
import functools

import jax
import jax.numpy as jnp
from jax import lax
from jax.experimental import pallas as pl
from jax.experimental.pallas import tpu as pltpu
from jax.sharding import PartitionSpec as P

ITERS = 3
LANES = 128
UP = 2
DOWN = 3
REACH = 2

in_stiff = 1.0
anchor_stiff = 0.25
cross_stiff = (0.25, 0.5, 0.5, 0.25)
reaches = (-2, -1, 1, 2)
MESH = pl.DeviceIdType.MESH


def pick(step, values):
    chosen = jnp.float32(values[-1])
    for index in range(len(values) - 1):
        chosen = jnp.where(step == index, jnp.float32(values[index]), chosen)
    return chosen


def kernel(
    n_sec, n_tile, off_ref, u_ref, v_in, frac_ref, fixed_ref, trans_ref, u_out, v_out,
    ext, ext_v, ext_f, keep, trans_all, anchor, part, part_tile, norms_sec, norms_tile,
    halo_send, halo_recv, tr_send, tr_recv, sec_send, sec_recv, tile_send, tile_recv,
):
    _, count, height, subs, lanes = u_ref.shape
    width = subs * lanes
    sections = count * n_sec
    rows = height * n_tile
    my_sec = lax.axis_index("sec")
    my_tile = lax.axis_index("tile")
    sec_first = my_sec * count
    row_first = my_tile * height
    shape = (height, subs, lanes)
    grow = row_first + lax.broadcasted_iota(jnp.int32, shape, 0)
    lane = lax.broadcasted_iota(jnp.int32, shape, 2)
    gcol = lax.broadcasted_iota(jnp.int32, shape, 1) * lanes + lane
    lane_of = lax.broadcasted_iota(jnp.int32, (1, 1, lanes), 2)

    ways = [(a, b) for a in (-1, 0, 1) for b in (-1, 0, 1) if (a, b) != (0, 0)]
    sec_at = {-1: pl.ds(REACH + count, REACH), 0: pl.ds(REACH, count), 1: pl.ds(0, REACH)}
    sec_from = {-1: pl.ds(REACH, REACH), 0: pl.ds(REACH, count), 1: pl.ds(count, REACH)}
    row_at = {-1: pl.ds(UP + height, DOWN), 0: pl.ds(UP, height), 1: pl.ds(0, UP)}
    row_from = {-1: pl.ds(UP, DOWN), 0: pl.ds(UP, height), 1: pl.ds(height, UP)}

    def halo(block, turn, way):
        a, b = ways[way]
        return pltpu.make_async_remote_copy(
            src_ref=block.at[:, sec_from[a], row_from[b]],
            dst_ref=block.at[:, sec_at[a], row_at[b]],
            send_sem=halo_send.at[turn, way],
            recv_sem=halo_recv.at[turn, way],
            device_id=(lax.rem(my_sec + a + n_sec, n_sec), lax.rem(my_tile + b + n_tile, n_tile)),
            device_id_type=MESH,
        )

    def there(a, b):
        sec_ok = (my_sec + a >= 0) & (my_sec + a < n_sec)
        return sec_ok & (my_tile + b >= 0) & (my_tile + b < n_tile)

    def send_halo(block, turn):
        for way, (a, b) in enumerate(ways):
            pl.when(there(a, b))(lambda way=way: halo(block, turn, way).start())

    def halo_sent(block, turn):
        for way, (a, b) in enumerate(ways):
            pl.when(there(a, b))(lambda way=way: halo(block, turn, way).wait_send())

    def halo_here(block, turn):
        for way, (a, b) in enumerate(ways):
            pl.when(there(-a, -b))(lambda way=way: halo(block, turn, way).wait_recv())

    def spread(src, slots, send, recv, n, me, peer):
        def copy(turn, place):
            return pltpu.make_async_remote_copy(
                src_ref=src,
                dst_ref=slots.at[place],
                send_sem=send.at[turn],
                recv_sem=recv.at[place],
                device_id=peer(lax.rem(me + turn, n)),
                device_id_type=MESH,
            )

        for turn in range(1, n):
            copy(turn, me).start()
        return copy

    def gathered(copy, n, me):
        for turn in range(1, n):
            copy(turn, lax.rem(me + turn, n)).wait_recv()
        for turn in range(1, n):
            copy(turn, me).wait_send()

    def along_sec(to):
        return (to, my_tile)

    def along_tile(to):
        return (my_sec, to)

    def shifted(cells, by):
        turned = pltpu.roll(cells, lax.rem(lanes - by, lanes), 2)
        after = pltpu.roll(turned, subs - 1, 1)
        before = pltpu.roll(turned, 1, 1)
        place = lane_of + by
        return jnp.where(place > lanes - 1, after, jnp.where(place < 0, before, turned))

    ext[:, REACH : REACH + count, UP : UP + height] = u_ref[...]
    send_halo(ext, 0)
    trans_copy = spread(trans_ref, trans_all, tr_send, tr_recv, n_sec, my_sec, along_sec)
    keep[...] = (1 - fixed_ref[...]).astype(jnp.float32)
    for c in range(2):
        ext_v[c, REACH : REACH + count, UP : UP + height] = v_in[c] * keep[...]
    send_halo(ext_v, 1)
    trans_all[my_sec] = trans_ref[...]
    gathered(trans_copy, n_sec, my_sec)
    before = jnp.zeros(trans_ref.shape, jnp.float32)
    for turn in range(n_sec):
        before = before + jnp.where(turn < my_sec, trans_all[turn], 0.0)
    for c in range(2):
        run = jnp.zeros((1, lanes), jnp.float32)
        for s in range(count):
            run = run + before[2 * s + c : 2 * s + c + 1]
        for s in range(count):
            run = run + trans_ref[2 * s + c : 2 * s + c + 1, :]
            anchor[2 * s + c : 2 * s + c + 1, :] = run

    halo_here(ext, 0)

    def iteration(step, _):
        ff = jnp.zeros((subs, lanes), jnp.float32)
        vv = jnp.zeros((subs, lanes), jnp.float32)
        for s in range(count):
            own = [ext[c, REACH + s, UP : UP + height] for c in range(2)]
            total = []
            for c in range(2):
                mid = own[c]
                above = ext[c, REACH + s, UP - 1 : UP - 1 + height]
                below = ext[c, REACH + s, UP + 1 : UP + 1 + height]
                f = jnp.where(grow > 0, above - mid, 0.0)
                f = f + jnp.where(grow < rows - 1, below - mid, 0.0)
                f = f + jnp.where(gcol > 0, shifted(mid, -1) - mid, 0.0)
                f = f + jnp.where(gcol < width - 1, shifted(mid, 1) - mid, 0.0)
                hold = anchor[2 * s + c : 2 * s + c + 1, :][None]
                total.append(in_stiff * f + anchor_stiff * (hold - mid))
            for j in range(4):
                reach = reaches[j]
                dr = off_ref[(j * count + s) * 2]
                dc = off_ref[(j * count + s) * 2 + 1]
                fr = frac_ref[0, j, s].astype(jnp.float32)
                fc = frac_ref[1, j, s].astype(jnp.float32)
                other = sec_first + s + reach
                least = jnp.where((other >= 0) & (other < sections), 0, rows + height)
                valid = (grow + dr >= least) & (grow + dr + 1 <= rows - 1)
                valid = valid & (gcol + dc >= 0) & (gcol + dc + 1 <= width - 1)
                flow = (dr.astype(jnp.float32) + fr, dc.astype(jnp.float32) + fc)
                for c in range(2):
                    near = ext[c, REACH + s + reach, pl.ds(UP + dr, height + 1)]
                    first = shifted(near, dc)
                    second = shifted(near, dc + 1)
                    top = first[:height] + fc * (second[:height] - first[:height])
                    low = first[1:] + fc * (second[1:] - first[1:])
                    match = top + fr * (low - top)
                    gap = match + flow[c] - own[c]
                    total[c] = total[c] + jnp.where(valid, cross_stiff[j] * gap, 0.0)
            for c in range(2):
                f = total[c] * keep[s]
                ext_f[step, c, REACH + s, UP : UP + height] = f
                v = ext_v[c, REACH + s, UP : UP + height]
                ff = ff + jnp.sum(f * f, 0)
                vv = vv + jnp.sum(v * v, 0)
        line = lax.broadcasted_iota(jnp.int32, (8, lanes), 0)
        ff = jnp.sum(ff, axis=0, keepdims=True)
        vv = jnp.sum(vv, axis=0, keepdims=True)
        mine = jnp.where(line == 0, ff, jnp.where(line == 1, vv, 0.0))
        part[step] = mine
        norms_sec[step, my_sec] = mine
        copy = spread(
            part.at[step], norms_sec.at[step], sec_send.at[step], sec_recv.at[step], n_sec, my_sec, along_sec
        )

        @pl.when(step < ITERS - 1)
        def _():
            send_halo(ext_f.at[step], 2 + step)

        @pl.when(step == 0)
        def _():
            halo_sent(ext, 0)
            halo_sent(ext_v, 1)
            halo_here(ext_v, 1)

        gathered(copy, n_sec, my_sec)
        summed = norms_sec[step, 0]
        for turn in range(1, n_sec):
            summed = summed + norms_sec[step, turn]
        part_tile[step] = summed
        norms_tile[step, my_tile] = summed
        copy = spread(
            part_tile.at[step], norms_tile.at[step], tile_send.at[step], tile_recv.at[step], n_tile, my_tile, along_tile
        )
        gathered(copy, n_tile, my_tile)
        summed = norms_tile[step, 0]
        for turn in range(1, n_tile):
            summed = summed + norms_tile[step, turn]
        all_ff = jnp.sum(summed[0:1], axis=(0, 1), keepdims=True)
        all_vv = jnp.sum(summed[1:2], axis=(0, 1), keepdims=True)
        ratio = jnp.sqrt(all_vv / (all_ff + 1e-06))
        alpha = pick(step, [0.1 * 0.99**k for k in range(ITERS)])
        delta = pick(step, [0.25 * 1.1**k for k in range(ITERS)])
        gain = jnp.broadcast_to(alpha * ratio + delta, (subs, lanes))[None]

        @pl.when(step < ITERS - 1)
        def _():
            halo_here(ext_f.at[step], 2 + step)
            halo_sent(ext_f.at[step], 2 + step)

        def advance(place, _):
            for c in range(2):
                v = (1.0 - alpha) * ext_v[c, place] + gain * ext_f[step, c, place]
                ext_v[c, place] = v
                ext[c, place] = ext[c, place] + delta * v
            return 0

        lax.fori_loop(0, count + 2 * REACH, advance, 0)
        return 0

    lax.fori_loop(0, ITERS, iteration, 0)
    u_out[...] = ext[:, REACH : REACH + count, UP : UP + height]
    v_out[...] = ext_v[:, REACH : REACH + count, UP : UP + height]


def shards(displacement, velocity, frac, offsets, fixed, trans):
    n_sec, n_tile = lax.axis_size("sec"), lax.axis_size("tile")
    _, count, height, width = displacement.shape
    subs = width // LANES
    cells = (2, count, height, subs, LANES)
    lines = -(-2 * count // 8) * 8
    shift = offsets[:, :, 0, :].reshape(-1)
    spread = jnp.broadcast_to(trans.reshape(-1, 1), (2 * count, LANES))
    spread = jnp.pad(spread, ((0, lines - 2 * count), (0, 0)))
    vmem = pl.BlockSpec(memory_space=pltpu.VMEM)
    dma = pltpu.SemaphoreType.DMA
    f32 = jnp.float32
    u, v = pl.pallas_call(
        functools.partial(kernel, n_sec, n_tile),
        out_shape=(jax.ShapeDtypeStruct(cells, f32), jax.ShapeDtypeStruct(cells, f32)),
        in_specs=[pl.BlockSpec(memory_space=pltpu.SMEM)] + [vmem] * 5,
        out_specs=(vmem, vmem),
        scratch_shapes=[
            pltpu.VMEM((2, count + 2 * REACH, height + UP + DOWN, subs, LANES), f32),
            pltpu.VMEM((2, count + 2 * REACH, height + UP + DOWN, subs, LANES), f32),
            pltpu.VMEM((ITERS, 2, count + 2 * REACH, height + UP + DOWN, subs, LANES), f32),
            pltpu.VMEM(cells[1:], f32),
            pltpu.VMEM((n_sec, lines, LANES), f32),
            pltpu.VMEM((lines, LANES), f32),
            pltpu.VMEM((ITERS, 8, LANES), f32),
            pltpu.VMEM((ITERS, 8, LANES), f32),
            pltpu.VMEM((ITERS, n_sec, 8, LANES), f32),
            pltpu.VMEM((ITERS, n_tile, 8, LANES), f32),
            dma((1 + ITERS, 8)),
            dma((1 + ITERS, 8)),
            dma((n_sec,)),
            dma((n_sec,)),
            dma((ITERS, n_sec)),
            dma((ITERS, n_sec)),
            dma((ITERS, n_tile)),
            dma((ITERS, n_tile)),
        ],
        compiler_params=pltpu.CompilerParams(has_side_effects=True, vmem_limit_bytes=40 * 2**20),
    )(
        shift,
        displacement.reshape(cells),
        velocity.reshape(cells),
        frac.reshape((2, 4) + cells[1:]),
        fixed.reshape(cells[1:]),
        spread,
    )
    return u.reshape(displacement.shape), v.reshape(displacement.shape)


def solution(mesh):
    placed = (
        P(None, "sec", "tile", None),
        P(None, "sec", "tile", None),
        P(None, None, "sec", "tile", None),
        P(None, "sec", "tile", None),
        P("sec", "tile", None),
        P("sec", None),
    )
    return jax.shard_map(
        shards,
        mesh=mesh,
        in_specs=placed,
        out_specs=(P(None, "sec", "tile", None), P(None, "sec", "tile", None)),
        check_vma=False,
    )
```

```python
import functools

import jax
import jax.numpy as jnp
from jax import lax
from jax.experimental import pallas as pl
from jax.experimental.pallas import tpu as pltpu
from jax.sharding import PartitionSpec as P

ITERS = 3
LANES = 128
UP = 2
DOWN = 3
REACH = 2

in_stiff = 1.0
anchor_stiff = 0.25
cross_stiff = (0.25, 0.5, 0.5, 0.25)
reaches = (-2, -1, 1, 2)
MESH = pl.DeviceIdType.MESH


def pick(step, values):
    chosen = jnp.float32(values[-1])
    for index in range(len(values) - 1):
        chosen = jnp.where(step == index, jnp.float32(values[index]), chosen)
    return chosen


def kernel(
    n_sec, n_tile, off_ref, u_ref, v_in, frac_ref, fixed_ref, trans_ref, u_out, v_out,
    ext, ext_v, ext_f, keep, trans_all, anchor, part, part_tile, norms_sec, norms_tile,
    halo_send, halo_recv, tr_send, tr_recv, sec_send, sec_recv, tile_send, tile_recv,
):
    _, count, height, subs, lanes = u_ref.shape
    width = subs * lanes
    sections = count * n_sec
    rows = height * n_tile
    my_sec = lax.axis_index("sec")
    my_tile = lax.axis_index("tile")
    sec_first = my_sec * count
    row_first = my_tile * height
    shape = (height, subs, lanes)
    grow = row_first + lax.broadcasted_iota(jnp.int32, shape, 0)
    lane = lax.broadcasted_iota(jnp.int32, shape, 2)
    gcol = lax.broadcasted_iota(jnp.int32, shape, 1) * lanes + lane
    lane_of = lax.broadcasted_iota(jnp.int32, (1, 1, lanes), 2)

    ways = [(a, b) for a in (-1, 0, 1) for b in (-1, 0, 1) if (a, b) != (0, 0)]
    sec_at = {-1: pl.ds(REACH + count, REACH), 0: pl.ds(REACH, count), 1: pl.ds(0, REACH)}
    sec_from = {-1: pl.ds(REACH, REACH), 0: pl.ds(REACH, count), 1: pl.ds(count, REACH)}
    row_at = {-1: pl.ds(UP + height, DOWN), 0: pl.ds(UP, height), 1: pl.ds(0, UP)}
    row_from = {-1: pl.ds(UP, DOWN), 0: pl.ds(UP, height), 1: pl.ds(height, UP)}

    def halo(block, turn, way):
        a, b = ways[way]
        return pltpu.make_async_remote_copy(
            src_ref=block.at[:, sec_from[a], row_from[b]],
            dst_ref=block.at[:, sec_at[a], row_at[b]],
            send_sem=halo_send.at[turn, way],
            recv_sem=halo_recv.at[turn, way],
            device_id=(lax.rem(my_sec + a + n_sec, n_sec), lax.rem(my_tile + b + n_tile, n_tile)),
            device_id_type=MESH,
        )

    def there(a, b):
        sec_ok = (my_sec + a >= 0) & (my_sec + a < n_sec)
        return sec_ok & (my_tile + b >= 0) & (my_tile + b < n_tile)

    def send_halo(block, turn):
        for way, (a, b) in enumerate(ways):
            pl.when(there(a, b))(lambda way=way: halo(block, turn, way).start())

    def halo_sent(block, turn):
        for way, (a, b) in enumerate(ways):
            pl.when(there(a, b))(lambda way=way: halo(block, turn, way).wait_send())

    def halo_here(block, turn):
        for way, (a, b) in enumerate(ways):
            pl.when(there(-a, -b))(lambda way=way: halo(block, turn, way).wait_recv())

    def spread(src, slots, send, recv, n, me, peer):
        def copy(turn, place):
            return pltpu.make_async_remote_copy(
                src_ref=src,
                dst_ref=slots.at[place],
                send_sem=send.at[turn],
                recv_sem=recv.at[place],
                device_id=peer(lax.rem(me + turn, n)),
                device_id_type=MESH,
            )

        for turn in range(1, n):
            copy(turn, me).start()
        return copy

    def gathered(copy, n, me):
        for turn in range(1, n):
            copy(turn, lax.rem(me + turn, n)).wait_recv()
        for turn in range(1, n):
            copy(turn, me).wait_send()

    def along_sec(to):
        return (to, my_tile)

    def along_tile(to):
        return (my_sec, to)

    def shifted(cells, by):
        turned = pltpu.roll(cells, lax.rem(lanes - by, lanes), 2)
        after = pltpu.roll(turned, subs - 1, 1)
        before = pltpu.roll(turned, 1, 1)
        place = lane_of + by
        return jnp.where(place > lanes - 1, after, jnp.where(place < 0, before, turned))

    ext[:, REACH : REACH + count, UP : UP + height] = u_ref[...]
    barrier = pltpu.get_barrier_semaphore()
    mates = [(lax.rem(my_sec + turn, n_sec), my_tile) for turn in range(1, n_sec)]
    mates += [(my_sec, lax.rem(my_tile + turn, n_tile)) for turn in range(1, n_tile)]
    for mate in mates:
        pl.semaphore_signal(barrier, inc=1, device_id=mate, device_id_type=MESH)
    corners = [(a, b) for a, b in ways if a != 0 and b != 0]
    for a, b in corners:
        def greet(a=a, b=b):
            pl.semaphore_signal(barrier, inc=1, device_id=(my_sec + a, my_tile + b), device_id_type=MESH)
        pl.when(there(a, b))(greet)
    met = len(mates) + sum(there(a, b).astype(jnp.int32) for a, b in corners)
    pl.semaphore_wait(barrier, met)
    send_halo(ext, 0)
    trans_copy = spread(trans_ref, trans_all, tr_send, tr_recv, n_sec, my_sec, along_sec)
    keep[...] = (1 - fixed_ref[...]).astype(jnp.float32)
    for c in range(2):
        ext_v[c, REACH : REACH + count, UP : UP + height] = v_in[c] * keep[...]
    send_halo(ext_v, 1)
    trans_all[my_sec] = trans_ref[...]
    gathered(trans_copy, n_sec, my_sec)
    before = jnp.zeros(trans_ref.shape, jnp.float32)
    for turn in range(n_sec):
        before = before + jnp.where(turn < my_sec, trans_all[turn], 0.0)
    for c in range(2):
        run = jnp.zeros((1, lanes), jnp.float32)
        for s in range(count):
            run = run + before[2 * s + c : 2 * s + c + 1]
        for s in range(count):
            run = run + trans_ref[2 * s + c : 2 * s + c + 1, :]
            anchor[2 * s + c : 2 * s + c + 1, :] = run

    halo_here(ext, 0)

    def iteration(step, _):
        ff = jnp.zeros((subs, lanes), jnp.float32)
        vv = jnp.zeros((subs, lanes), jnp.float32)
        for s in range(count):
            own = [ext[c, REACH + s, UP : UP + height] for c in range(2)]
            total = []
            for c in range(2):
                mid = own[c]
                above = ext[c, REACH + s, UP - 1 : UP - 1 + height]
                below = ext[c, REACH + s, UP + 1 : UP + 1 + height]
                f = jnp.where(grow > 0, above - mid, 0.0)
                f = f + jnp.where(grow < rows - 1, below - mid, 0.0)
                f = f + jnp.where(gcol > 0, shifted(mid, -1) - mid, 0.0)
                f = f + jnp.where(gcol < width - 1, shifted(mid, 1) - mid, 0.0)
                hold = anchor[2 * s + c : 2 * s + c + 1, :][None]
                total.append(in_stiff * f + anchor_stiff * (hold - mid))
            for j in range(4):
                reach = reaches[j]
                dr = off_ref[(j * count + s) * 2]
                dc = off_ref[(j * count + s) * 2 + 1]
                fr = frac_ref[0, j, s].astype(jnp.float32)
                fc = frac_ref[1, j, s].astype(jnp.float32)
                other = sec_first + s + reach
                least = jnp.where((other >= 0) & (other < sections), 0, rows + height)
                valid = (grow + dr >= least) & (grow + dr + 1 <= rows - 1)
                valid = valid & (gcol + dc >= 0) & (gcol + dc + 1 <= width - 1)
                flow = (dr.astype(jnp.float32) + fr, dc.astype(jnp.float32) + fc)
                for c in range(2):
                    near = ext[c, REACH + s + reach, pl.ds(UP + dr, height + 1)]
                    first = shifted(near, dc)
                    second = shifted(near, dc + 1)
                    top = first[:height] + fc * (second[:height] - first[:height])
                    low = first[1:] + fc * (second[1:] - first[1:])
                    match = top + fr * (low - top)
                    gap = match + flow[c] - own[c]
                    total[c] = total[c] + jnp.where(valid, cross_stiff[j] * gap, 0.0)
            for c in range(2):
                f = total[c] * keep[s]
                ext_f[step, c, REACH + s, UP : UP + height] = f
                v = ext_v[c, REACH + s, UP : UP + height]
                ff = ff + jnp.sum(f * f, 0)
                vv = vv + jnp.sum(v * v, 0)
        line = lax.broadcasted_iota(jnp.int32, (8, lanes), 0)
        ff = jnp.sum(ff, axis=0, keepdims=True)
        vv = jnp.sum(vv, axis=0, keepdims=True)
        mine = jnp.where(line == 0, ff, jnp.where(line == 1, vv, 0.0))
        part[step] = mine
        norms_sec[step, my_sec] = mine
        copy = spread(
            part.at[step], norms_sec.at[step], sec_send.at[step], sec_recv.at[step], n_sec, my_sec, along_sec
        )

        @pl.when(step < ITERS - 1)
        def _():
            send_halo(ext_f.at[step], 2 + step)

        @pl.when(step == 0)
        def _():
            halo_sent(ext, 0)
            halo_sent(ext_v, 1)
            halo_here(ext_v, 1)

        gathered(copy, n_sec, my_sec)
        summed = norms_sec[step, 0]
        for turn in range(1, n_sec):
            summed = summed + norms_sec[step, turn]
        part_tile[step] = summed
        norms_tile[step, my_tile] = summed
        copy = spread(
            part_tile.at[step], norms_tile.at[step], tile_send.at[step], tile_recv.at[step], n_tile, my_tile, along_tile
        )
        gathered(copy, n_tile, my_tile)
        summed = norms_tile[step, 0]
        for turn in range(1, n_tile):
            summed = summed + norms_tile[step, turn]
        all_ff = jnp.sum(summed[0:1], axis=(0, 1), keepdims=True)
        all_vv = jnp.sum(summed[1:2], axis=(0, 1), keepdims=True)
        ratio = jnp.sqrt(all_vv / (all_ff + 1e-06))
        alpha = pick(step, [0.1 * 0.99**k for k in range(ITERS)])
        delta = pick(step, [0.25 * 1.1**k for k in range(ITERS)])
        gain = jnp.broadcast_to(alpha * ratio + delta, (subs, lanes))[None]

        @pl.when(step < ITERS - 1)
        def _():
            halo_here(ext_f.at[step], 2 + step)
            halo_sent(ext_f.at[step], 2 + step)

        def advance(place, _):
            for c in range(2):
                v = (1.0 - alpha) * ext_v[c, place] + gain * ext_f[step, c, place]
                ext_v[c, place] = v
                ext[c, place] = ext[c, place] + delta * v
            return 0

        lax.fori_loop(0, count + 2 * REACH, advance, 0)
        return 0

    lax.fori_loop(0, ITERS, iteration, 0)
    u_out[...] = ext[:, REACH : REACH + count, UP : UP + height]
    v_out[...] = ext_v[:, REACH : REACH + count, UP : UP + height]


def shards(displacement, velocity, frac, offsets, fixed, trans):
    n_sec, n_tile = lax.axis_size("sec"), lax.axis_size("tile")
    _, count, height, width = displacement.shape
    subs = width // LANES
    cells = (2, count, height, subs, LANES)
    lines = -(-2 * count // 8) * 8
    shift = offsets[:, :, 0, :].reshape(-1)
    spread = jnp.broadcast_to(trans.reshape(-1, 1), (2 * count, LANES))
    spread = jnp.pad(spread, ((0, lines - 2 * count), (0, 0)))
    vmem = pl.BlockSpec(memory_space=pltpu.VMEM)
    dma = pltpu.SemaphoreType.DMA
    f32 = jnp.float32
    u, v = pl.pallas_call(
        functools.partial(kernel, n_sec, n_tile),
        out_shape=(jax.ShapeDtypeStruct(cells, f32), jax.ShapeDtypeStruct(cells, f32)),
        in_specs=[pl.BlockSpec(memory_space=pltpu.SMEM)] + [vmem] * 5,
        out_specs=(vmem, vmem),
        scratch_shapes=[
            pltpu.VMEM((2, count + 2 * REACH, height + UP + DOWN, subs, LANES), f32),
            pltpu.VMEM((2, count + 2 * REACH, height + UP + DOWN, subs, LANES), f32),
            pltpu.VMEM((ITERS, 2, count + 2 * REACH, height + UP + DOWN, subs, LANES), f32),
            pltpu.VMEM(cells[1:], f32),
            pltpu.VMEM((n_sec, lines, LANES), f32),
            pltpu.VMEM((lines, LANES), f32),
            pltpu.VMEM((ITERS, 8, LANES), f32),
            pltpu.VMEM((ITERS, 8, LANES), f32),
            pltpu.VMEM((ITERS, n_sec, 8, LANES), f32),
            pltpu.VMEM((ITERS, n_tile, 8, LANES), f32),
            dma((1 + ITERS, 8)),
            dma((1 + ITERS, 8)),
            dma((n_sec,)),
            dma((n_sec,)),
            dma((ITERS, n_sec)),
            dma((ITERS, n_sec)),
            dma((ITERS, n_tile)),
            dma((ITERS, n_tile)),
        ],
        compiler_params=pltpu.CompilerParams(collective_id=0, has_side_effects=True, vmem_limit_bytes=40 * 2**20),
    )(
        shift,
        displacement.reshape(cells),
        velocity.reshape(cells),
        frac.reshape((2, 4) + cells[1:]),
        fixed.reshape(cells[1:]),
        spread,
    )
    return u.reshape(displacement.shape), v.reshape(displacement.shape)


def solution(mesh):
    placed = (
        P(None, "sec", "tile", None),
        P(None, "sec", "tile", None),
        P(None, None, "sec", "tile", None),
        P(None, "sec", "tile", None),
        P("sec", "tile", None),
        P("sec", None),
    )
    return jax.shard_map(
        shards,
        mesh=mesh,
        in_specs=placed,
        out_specs=(P(None, "sec", "tile", None), P(None, "sec", "tile", None)),
        check_vma=False,
    )
```
